32 devices in a mesh: groups: 2 (over y), frames: 4 (over z), rows: 2 (over x), heads: 2 (over core).
Axes of the slice: x: 2, y: 2, z: 4, core: 2. Of those that a mesh axis runs over, the one named last changes fastest.
Arguments:
- clip_latent: bfloat16 [8, 12, 48, 640], P(('groups', 'frames'), 'rows', None, 'heads'), parts along dimension 0, may hold values from -40 to 40, as said below
- norm_gain: float32 [640], replicated, may hold values from 0.1 to 1.9
- w_time: bfloat16 [3, 640, 640], replicated, may hold values from -0.125 to 0.125
- w_query: bfloat16 [640, 640], P(None, 'heads'), may hold values from -0.7109375 to 0.7109375
- w_key: bfloat16 [640, 640], P(None, 'heads'), may hold values from -0.25 to 0.25
- w_value: bfloat16 [640, 640], P(None, 'heads'), may hold values from -0.25 to 0.25
- w_out: bfloat16 [640, 640], P('heads'), may hold values from -0.25 to 0.25
- reference_tokens: bfloat16 [288, 640], P(('groups', 'frames', 'rows'), 'heads'), parts along dimension 0, may hold values from -160 to 160, as said below
Outputs:
- block_out: bfloat16 [8, 12, 48, 640], P(('groups', 'frames'), 'rows', None, 'heads'), parts along dimension 0
The draws below stay inside these ranges and needn't reach their ends.
There are 2 independent parts, one for each index of `groups`. The reference program is written for one: setup_inputs(seed, part) draws one part's arguments, and reference() takes and returns one part's arrays. A program takes and returns all parts, laid end to end along the dimension named above; an argument that names none is the same for every part. Nothing has to cross between parts.
Inputs may be any that keep to these rules, and one draw needn't show every extreme that they name: `clip_latent`: Real-valued latent features; each channel and each position has its own scale. `reference_tokens`: Real-valued reference features.
All inputs are finite; a program needn't handle non-finite values.
Results may differ from the reference program's by a relative error of at most 0.022.
Values may be sent and summed in bfloat16 or wider, within the bound.
No kernel may reach another device: no remote copies, remote signals or barrier semaphores. Data moves between devices by JAX's collectives and lax.ppermute only.
A program may use at most 64 MiB of HBM per device.

```python
import math
import jax
import jax.numpy as jnp
from jax import lax

C = 640
HEADS = 8
FRAMES = 4
LH = 12
LW = 48
RT = 144


def draw_clip_latent(key, part):
    keys = jax.random.split(jax.random.fold_in(key, 11), 3)
    chan_scale = jnp.exp(jax.random.uniform(keys[0], (C,), jnp.float32, 0.0, math.log(3.2)))
    tok_scale = jnp.exp(jax.random.uniform(keys[1], (FRAMES, LH, LW, 1), jnp.float32, 0.0, math.log(3.2)))
    base = jax.random.normal(keys[2], (FRAMES, LH, LW, C), jnp.float32)
    return jnp.clip(base * chan_scale * tok_scale, -40.0, 40.0).astype(jnp.bfloat16)


def draw_reference_tokens(key, part):
    keys = jax.random.split(jax.random.fold_in(key, 23), 3)
    base = jax.random.normal(keys[2], (RT, C), jnp.float32)
    return jnp.clip(base, -6.0, 6.0).astype(jnp.bfloat16)


def steps_of(key, shape, cuts, least, top_value):
    def one(dim, blocks):
        heights = jax.random.uniform(jax.random.fold_in(jax.random.fold_in(key, 6), dim), (blocks,), jnp.float32, least / len(cuts), top_value / len(cuts))
        return jnp.repeat(jnp.exp(heights), shape[dim] // blocks).reshape((-1,) + (1,) * (len(shape) - dim - 1))

    loudness = one(*cuts[0])
    for cut in cuts[1:]:
        loudness = loudness * one(*cut)
    return loudness


def bell_draw(rng, shape, scale, limit, shards=(), kind=jnp.bfloat16):
    entries = scale * jax.random.normal(rng, shape, jnp.float32)
    if shards:
        entries = entries * steps_of(rng, shape, shards, -0.22, 0.18)
    return jnp.clip(entries, -limit, limit).astype(kind)


def setup_inputs(seed: int = 0, part: int = 0) -> dict:
    key_list = jax.random.split(jax.random.key(seed), 9)
    own_keys = jax.random.split(jax.random.fold_in(key_list[8], part), 9)
    clip_latent = draw_clip_latent(jax.random.fold_in(jax.random.fold_in(key_list[8], part), 71), part)
    norm_gain = jnp.clip(1.0 + 0.18 * jax.random.normal(key_list[1], (C,), jnp.float32), 0.1, 1.9)
    w_time = bell_draw(key_list[2], (3, C, C), (3 * C) ** -0.5, 0.125)
    w_query = bell_draw(key_list[3], (C, C), (3.0 * C ** -0.5), 0.7109375, ((1, 2),))
    w_key = bell_draw(key_list[4], (C, C), C ** -0.5, 0.25, ((1, 2),))
    w_value = bell_draw(key_list[5], (C, C), C ** -0.5, 0.25, ((1, 2),))
    w_out = bell_draw(key_list[6], (C, C), C ** -0.5, 0.25, ((0, 2),))
    reference_tokens = draw_reference_tokens(jax.random.fold_in(jax.random.fold_in(key_list[8], part), 71), part)
    return dict(clip_latent=clip_latent, norm_gain=norm_gain, w_time=w_time, w_query=w_query, w_key=w_key, w_value=w_value, w_out=w_out, reference_tokens=reference_tokens)


def attend_head(operands):
    query_head, key_head, value_head = operands
    scores = jnp.dot(query_head, key_head.T, preferred_element_type=jnp.float32)
    top = lax.optimization_barrier(jnp.max(scores, axis=1, keepdims=True))
    expo = jnp.exp(scores - top)
    total = lax.optimization_barrier(jnp.sum(expo, axis=1, keepdims=True))
    probs = expo.astype(jnp.bfloat16)
    return (jnp.dot(probs, value_head, preferred_element_type=jnp.float32) / total).astype(jnp.bfloat16)

def reference(clip_latent, norm_gain, w_time, w_query, w_key, w_value, w_out, reference_tokens):
    frames_all = clip_latent.shape[0]
    head_size = C // HEADS
    padded = jnp.pad(clip_latent, ((1, 1), (0, 0), (0, 0), (0, 0)))
    summed = jnp.dot(padded[0:frames_all], w_time[0], preferred_element_type=jnp.float32)
    summed = summed + jnp.dot(padded[1:1 + frames_all], w_time[1], preferred_element_type=jnp.float32)
    summed = summed + jnp.dot(padded[2:2 + frames_all], w_time[2], preferred_element_type=jnp.float32)
    temporal = (clip_latent.astype(jnp.float32) + summed).astype(jnp.bfloat16)
    feats = temporal.astype(jnp.float32)
    centre = lax.optimization_barrier(jnp.mean(feats, axis=-1, keepdims=True))
    spread = lax.optimization_barrier(jnp.mean((feats - centre) ** 2, axis=-1, keepdims=True))
    normed = ((feats - centre) * lax.rsqrt(spread + 1e-05) * norm_gain).astype(jnp.bfloat16)
    scale = 1.0 / jnp.sqrt(jnp.float32(head_size))
    query = (jnp.dot(normed, w_query, preferred_element_type=jnp.float32) * scale).astype(jnp.bfloat16)
    keys = jnp.dot(reference_tokens, w_key, preferred_element_type=jnp.float32).astype(jnp.bfloat16)
    values = jnp.dot(reference_tokens, w_value, preferred_element_type=jnp.float32).astype(jnp.bfloat16)
    key_heads = keys.reshape(-1, HEADS, head_size).transpose(1, 0, 2)
    value_heads = values.reshape(-1, HEADS, head_size).transpose(1, 0, 2)

    def per_frame(query_frame):
        rows_here, cols_here, chans = query_frame.shape
        query_heads = query_frame.reshape(-1, HEADS, head_size).transpose(1, 0, 2)
        result = lax.map(attend_head, (query_heads, key_heads, value_heads))
        return result.transpose(1, 0, 2).reshape(rows_here, cols_here, chans)
    attended = lax.map(per_frame, query)
    mixed = jnp.dot(attended, w_out, preferred_element_type=jnp.float32)
    return (temporal.astype(jnp.float32) + mixed).astype(jnp.bfloat16)
```

```python
import functools

import jax
import jax.numpy as jnp
from jax import lax
from jax.experimental import pallas as pl
from jax.experimental.pallas import tpu as pltpu
from jax.sharding import PartitionSpec as P

C = 640
HEADS = 8
EPS = 1e-05

F32 = jnp.float32
BF16 = jnp.bfloat16


def nt_dot(a, b):
    return lax.dot_general(a, b, (((1,), (1,)), ((), ())), preferred_element_type=F32)


def tn_dot(a, b):
    return lax.dot_general(a, b, (((0,), (0,)), ((), ())), preferred_element_type=F32)


def sibling(x):
    return lax.ppermute(x, "heads", [(0, 1), (1, 0)])


def frame_pairs(x):
    count = lax.axis_size("frames")
    perm = []
    for core in range(2):
        for low in range(core, count - 1, 2):
            perm.append((low * 2 + core, (low + 1) * 2 + core))
            perm.append(((low + 1) * 2 + core, low * 2 + core))
    return lax.ppermute(x, ("frames", "heads"), perm)


def gather_blocks(x, axis):
    count = lax.axis_size(axis)
    if count & (count - 1):
        return lax.all_gather(x, axis, axis=0, tiled=True)
    step = 1
    while step < count:
        other = lax.ppermute(x, axis, [(i, i ^ step) for i in range(count)])
        x = jnp.concatenate([x, other], axis=0)
        step *= 2
    return x


def join_halves(core, own, other):
    first = jnp.where(core == 0, own, other)
    second = jnp.where(core == 0, other, own)
    return jnp.concatenate([first, second], axis=-1)


def middle_kernel(full_ref, w_ref, acc_ref):
    full = full_ref[...]
    acc_ref[...] = full.astype(F32) + jnp.dot(full, w_ref[1], preferred_element_type=F32)


def query_kernel(acc_ref, own_ref, other_ref, w_ref, wq_own_ref, wq_other_ref, gain_ref, temporal_ref, query_ref):
    core = lax.axis_index("heads")
    frame = lax.axis_index("frames")
    tap = jnp.where(lax.rem(frame, 2) == core, 2, 0)
    summed = acc_ref[...]
    summed = summed + jnp.dot(own_ref[...], w_ref[tap], preferred_element_type=F32)
    summed = summed + jnp.dot(other_ref[...], w_ref[2 - tap], preferred_element_type=F32)
    temporal = summed.astype(BF16)
    temporal_ref[...] = temporal
    feats = temporal.astype(F32)
    centre = jnp.mean(feats, axis=-1, keepdims=True)
    centred = feats - centre
    spread = jnp.mean(centred * centred, axis=-1, keepdims=True)
    normed = (centred * lax.rsqrt(spread + EPS) * gain_ref[...]).astype(BF16)
    scale = (C // HEADS) ** -0.5
    half = wq_own_ref.shape[0]
    query_ref[:half] = (nt_dot(wq_own_ref[...], normed) * scale).astype(BF16)
    query_ref[half:] = (nt_dot(wq_other_ref[...], normed) * scale).astype(BF16)


def attend_kernel(
    tok_ref, query_ref, temporal_ref, wk_own_ref, wk_other_ref, wv_own_ref, wv_other_ref, wo_own_ref, wo_other_ref,
    out_ref, tokens, attended,
):
    core = lax.axis_index("heads")
    blocks, width, _ = tok_ref.shape
    for i in range(blocks):
        tokens[i * width : (i + 1) * width] = tok_ref[i]
    toks = tokens[...].astype(BF16)
    size = C // HEADS
    half = wk_own_ref.shape[0]
    for part, (wk_ref, wv_ref) in enumerate(((wk_own_ref, wv_own_ref), (wk_other_ref, wv_other_ref))):
        values = nt_dot(wv_ref[...], toks).astype(BF16)
        for head in range(half // size):
            rows = slice(head * size, (head + 1) * size)
            keys = nt_dot(toks, wk_ref[rows]).astype(BF16)
            at = part * half + head * size
            scores = jnp.dot(keys, query_ref[at : at + size], preferred_element_type=F32)
            expo = jnp.exp(scores - jnp.max(scores, axis=0, keepdims=True))
            total = jnp.sum(expo, axis=0, keepdims=True)
            mixed = jnp.dot(values[rows], expo.astype(BF16), preferred_element_type=F32)
            attended[at : at + size] = (mixed / total).astype(BF16)
    mixed = tn_dot(attended[:half], wo_own_ref[...]) + tn_dot(attended[half:], wo_other_ref[...])
    mixed = temporal_ref[...].astype(F32) + mixed
    out_ref[...] = jnp.where(core == 0, mixed[:, :half], mixed[:, half:]).astype(BF16)


VMEM = pl.BlockSpec(memory_space=pltpu.VMEM)


def call(kernel, operands, outs, scratch=(), flops=0):
    return pl.pallas_call(
        kernel,
        out_shape=[jax.ShapeDtypeStruct(shape, dtype) for shape, dtype in outs],
        in_specs=[VMEM] * len(operands),
        out_specs=[VMEM] * len(outs),
        scratch_shapes=list(scratch),
        compiler_params=pltpu.CompilerParams(vmem_limit_bytes=48 * 2**20),
        cost_estimate=pl.CostEstimate(
            flops=flops, bytes_accessed=sum(x.size * x.dtype.itemsize for x in operands), transcendentals=0
        ),
    )(*operands)


def body(clip_latent, norm_gain, w_time, w_query, w_key, w_value, w_out, reference_tokens):
    frames_here, rows_here, cols_here, half = clip_latent.shape
    assert frames_here == 1 and lax.axis_size("heads") == 2
    core = lax.axis_index("heads")
    places = rows_here * cols_here
    clip = clip_latent.reshape(places, half)
    full = join_halves(core, clip, sibling(clip))
    near = frame_pairs(full)
    wq, wk, wv = w_query.T, w_key.T, w_value.T
    wq_other, wk_other, wv_other, wo_other = sibling(wq), sibling(wk), sibling(wv), sibling(w_out)
    toks = gather_blocks(gather_blocks(reference_tokens[None], "rows"), "frames")
    toks = join_halves(core, toks, sibling(toks))
    near_other = sibling(near)
    (acc,) = call(middle_kernel, (full, w_time), [((places, C), F32)], flops=2 * places * C * C)
    temporal, query = call(
        query_kernel,
        (acc, near, near_other, w_time, wq, wq_other, norm_gain[None]),
        [((places, C), BF16), ((C, places), BF16)],
        flops=6 * places * C * C,
    )
    count = toks.shape[0] * toks.shape[1]
    (out,) = call(
        attend_kernel,
        (toks, query, temporal, wk, wk_other, wv, wv_other, w_out, wo_other),
        [((places, half), BF16)],
        [pltpu.VMEM((count, C), BF16), pltpu.VMEM((C, places), BF16)],
        flops=4 * places * count * C + 2 * places * C * C + 4 * count * C * C,
    )
    return out.reshape(clip_latent.shape)


def solution(mesh):
    return jax.shard_map(
        body,
        mesh=mesh,
        in_specs=(
            P(("groups", "frames"), "rows", None, "heads"),
            P(),
            P(),
            P(None, "heads"),
            P(None, "heads"),
            P(None, "heads"),
            P("heads", None),
            P(("groups", "frames", "rows"), "heads"),
        ),
        out_specs=P(("groups", "frames"), "rows", None, "heads"),
        check_vma=False,
    )
```

```python
import functools

import jax
import jax.numpy as jnp
from jax import lax
from jax.experimental import pallas as pl
from jax.experimental.pallas import tpu as pltpu
from jax.sharding import PartitionSpec as P

C = 640
HEADS = 8
EPS = 1e-05

PACK, SHARE, FAR = 10**9, 10**9, 5 * 10**9
MIDDLE, FIRST, SECOND, QUERY, ATTEND = 5 * 10**8, 5 * 10**8, 3 * 10**8, 10**9, 2 * 10**9

F32 = jnp.float32
BF16 = jnp.bfloat16


def nt_dot(a, b):
    return lax.dot_general(a, b, (((1,), (1,)), ((), ())), preferred_element_type=F32)


def tn_dot(a, b):
    return lax.dot_general(a, b, (((0,), (0,)), ((), ())), preferred_element_type=F32)


def sibling(x):
    return lax.ppermute(x, "heads", [(0, 1), (1, 0)])


def swap(x, partner):
    frames, rows = lax.axis_size("frames"), lax.axis_size("rows")
    perm = []
    for frame in range(frames):
        for row in range(rows):
            for core in range(2):
                to = partner(frame, row, core)
                if to is not None:
                    perm.append((((frame * rows) + row) * 2 + core, ((to[0] * rows) + to[1]) * 2 + to[2]))
    return lax.ppermute(x, ("frames", "rows", "heads"), perm)


def swap_near(x):
    frames, rows = lax.axis_size("frames"), lax.axis_size("rows")

    def partner(frame, row, core):
        to = frame + 1 if frame % 2 == core else frame - 1
        if 0 <= to < frames:
            return to, row, core
        return (frame, row ^ 1, core) if rows % 2 == 0 else None

    return swap(x, partner)


def swap_far(x):
    return swap(x, lambda frame, row, core: (frame ^ (3 if core else 2), row, core))


def swap_bit(x, axis, bit):
    return lax.ppermute(x, axis, [(i, i ^ bit) for i in range(lax.axis_size(axis))])


VMEM = pl.BlockSpec(memory_space=pltpu.VMEM)


def call(kernel, operands, outs, scratch=(), flops=0):
    return pl.pallas_call(
        kernel,
        out_shape=[jax.ShapeDtypeStruct(shape, dtype) for shape, dtype in outs],
        in_specs=[VMEM] * len(operands),
        out_specs=[VMEM] * len(outs),
        scratch_shapes=list(scratch),
        compiler_params=pltpu.CompilerParams(vmem_limit_bytes=40 * 2**20),
        cost_estimate=pl.CostEstimate(flops=flops, bytes_accessed=0, transcendentals=0),
    )(*operands)


def pack_kernel(clip_other_ref, tok_ref, tok_other_ref, message_ref, pair_ref):
    places, width = clip_other_ref.shape[0], tok_ref.shape[0]
    message_ref[:places] = clip_other_ref[...]
    message_ref[places : places + width] = pair_ref[0] = tok_ref[...]
    message_ref[places + width :] = pair_ref[1] = tok_other_ref[...]


def stack_kernel(*refs):
    at = 0
    for ref in refs[:-1]:
        refs[-1][at : at + ref.shape[0]] = ref[...]
        at += ref.shape[0]


def stack(*parts, flops):
    shape = (sum(part.shape[0] for part in parts),) + parts[0].shape[1:]
    return call(stack_kernel, parts, [(shape, BF16)], flops=flops)[0]


def share_kernel(frames, pair_ref, near_ref, far_ref, out_ref):
    core = lax.axis_index("heads")
    frame = lax.axis_index("frames")
    edge = (frame == 0) | (frame == frames - 1)
    width = pair_ref.shape[1]
    places = near_ref.shape[0] - 2 * width
    for side in range(2):
        near = near_ref[places + side * width : places + (side + 1) * width]
        out_ref[side] = jnp.where(core == 0, near, pair_ref[side])
        out_ref[2 + side] = jnp.where((core == 0) | edge, far_ref[side], near)


def gather_tokens(pair, near):
    frames, rows = lax.axis_size("frames"), lax.axis_size("rows")
    if frames == 4 and rows == 2:
        far = stack(swap_far(pair), flops=FAR)
        (mine,) = call(
            functools.partial(share_kernel, frames),
            (pair, near, far),
            [((4,) + pair.shape[1:], BF16)],
            flops=SHARE,
        )
        met = swap_bit(mine, "rows", 1)
        return [(mine, False), (sibling(mine), True), (met, False), (sibling(met), True)]
    parts = [pair]
    for axis, count in (("frames", frames), ("rows", rows)):
        assert count & (count - 1) == 0
        bit = 1
        while bit < count:
            held = stack(*parts, flops=SHARE)
            parts = [held, swap_bit(held, axis, bit)]
            bit *= 2
    return [(part, False) for part in parts]


def halves(core, half):
    own = pl.multiple_of(core * half, 16)
    return pl.ds(own, half), pl.ds(pl.multiple_of(half - own, 16), half)


def beside(near_ref, places, core, frames):
    frame = lax.axis_index("frames")
    after = lax.rem(frame, 2) == core
    there = jnp.where(after, frame < frames - 1, frame > 0)
    near = near_ref[:places]
    return jnp.where(there, near, jnp.zeros_like(near)), jnp.where(after, 2, 0)


def middle_kernel(own_ref, other_ref, w_ref, wo_own_ref, wo_other_ref, acc_ref, wo_ref, full):
    core = lax.axis_index("heads")
    half = wo_own_ref.shape[0]
    own, other = own_ref[...], other_ref[...]
    full[:, :half] = jnp.where(core == 0, own, other)
    full[:, half:] = jnp.where(core == 0, other, own)
    whole = full[...]
    acc_ref[...] = whole.astype(F32) + jnp.dot(whole, w_ref[1], preferred_element_type=F32)
    wo_ref[:half] = jnp.where(core == 0, wo_own_ref[:, :half], wo_own_ref[:, half:])
    wo_ref[half:] = jnp.where(core == 0, wo_other_ref[:, :half], wo_other_ref[:, half:])


def first_kernel(frames, acc_ref, near_ref, near_other_ref, w_ref, sum_ref):
    core = lax.axis_index("heads")
    places = acc_ref.shape[0]
    own, other = halves(core, near_ref.shape[1])
    near, tap = beside(near_ref, places, core, frames)
    sums = acc_ref[...] + jnp.dot(near, w_ref[tap, own], preferred_element_type=F32)
    near, tap = beside(near_other_ref, places, 1 - core, frames)
    sum_ref[...] = sums + jnp.dot(near, w_ref[tap, other], preferred_element_type=F32)


def second_kernel(frames, acc_ref, near_ref, w_ref, sum_ref):
    core = lax.axis_index("heads")
    near, tap = beside(near_ref, acc_ref.shape[0], core, frames)
    other = halves(core, near_ref.shape[1])[1]
    sum_ref[...] = acc_ref[...] + jnp.dot(near, w_ref[tap, other], preferred_element_type=F32)


def query_kernel(frames, acc_ref, near_ref, w_ref, wq_own_ref, wq_other_ref, gain_ref, temporal_ref, query_ref):
    core = lax.axis_index("heads")
    half = wq_own_ref.shape[0]
    near, tap = beside(near_ref, acc_ref.shape[0], 1 - core, frames)
    own = halves(core, half)[0]
    temporal = (acc_ref[...] + jnp.dot(near, w_ref[tap, own], preferred_element_type=F32)).astype(BF16)
    temporal_ref[...] = jnp.where(core == 0, temporal[:, :half], temporal[:, half:])
    feats = temporal.astype(F32)
    centre = jnp.mean(feats, axis=-1, keepdims=True)
    centred = feats - centre
    spread = jnp.mean(centred * centred, axis=-1, keepdims=True)
    normed = (centred * lax.rsqrt(spread + EPS) * gain_ref[...]).astype(BF16)
    scale = (C // HEADS) ** -0.5
    query_ref[:half] = (nt_dot(wq_own_ref[...], normed) * scale).astype(BF16)
    query_ref[half:] = (nt_dot(wq_other_ref[...], normed) * scale).astype(BF16)


def attend_kernel(flipped, *refs):
    core = lax.axis_index("heads")
    blocks, refs = refs[: len(flipped)], refs[len(flipped) :]
    query_ref, temporal_ref, wk_own_ref, wk_other_ref, wv_own_ref, wv_other_ref, wo_ref = refs[:7]
    out_ref, tokens, keys, values, attended = refs[7:]
    half = wk_own_ref.shape[0]
    size = C // HEADS
    at = 0
    for ref, flip in zip(blocks, flipped):
        for i in range(0, ref.shape[0], 2):
            first, second = (ref[i + 1], ref[i]) if flip else (ref[i], ref[i + 1])
            rows = slice(at, at + ref.shape[1])
            tokens[rows, :half] = jnp.where(core == 0, first, second)
            tokens[rows, half:] = jnp.where(core == 0, second, first)
            at += ref.shape[1]
    toks = tokens[...]
    for part, (wk_ref, wv_ref) in enumerate(((wk_own_ref, wv_own_ref), (wk_other_ref, wv_other_ref))):
        values[part * half : (part + 1) * half] = nt_dot(wv_ref[...], toks).astype(BF16)
        found = nt_dot(toks, wk_ref[...]).astype(BF16)
        for head in range(half // size):
            keys[part * (half // size) + head, :, :size] = found[:, head * size : (head + 1) * size]
    probs = []
    for head in range(HEADS):
        rows = slice(head * size, (head + 1) * size)
        scores = jnp.dot(keys[head, :, :size], query_ref[rows], preferred_element_type=F32)
        expo = jnp.exp(scores - jnp.max(scores, axis=0, keepdims=True))
        probs.append((expo.astype(BF16), 1.0 / jnp.sum(expo, axis=0, keepdims=True)))
    for head in range(HEADS):
        rows = slice(head * size, (head + 1) * size)
        prob, inverse = probs[head]
        mixed = jnp.dot(values[rows], prob, preferred_element_type=F32)
        attended[rows] = (mixed * inverse).astype(BF16)
    mixed = tn_dot(attended[...], wo_ref[...])
    out_ref[...] = (temporal_ref[...].astype(F32) + mixed).astype(BF16)


def body(clip_latent, norm_gain, w_time, w_query, w_key, w_value, w_out, reference_tokens):
    frames_here, rows_here, cols_here, half = clip_latent.shape
    assert frames_here == 1 and lax.axis_size("heads") == 2
    places = rows_here * cols_here
    width = reference_tokens.shape[0]
    clip = clip_latent.reshape(places, half)
    frames = lax.axis_size("frames")
    clip_other, toks_other = sibling(clip), sibling(reference_tokens)
    near = swap_near(clip)
    message, pair = call(
        pack_kernel,
        (clip_other, reference_tokens, toks_other),
        [((places + 2 * width, half), BF16), ((2, width, half), BF16)],
        flops=PACK,
    )
    late = swap_near(message)
    near_other, late_other = sibling(near), sibling(late)
    toks = gather_tokens(pair, late)
    wq, wk, wv = w_query.T, w_key.T, w_value.T
    wq_other, wk_other, wv_other, wo_other = sibling(wq), sibling(wk), sibling(wv), sibling(w_out)
    acc, wo = call(
        middle_kernel,
        (clip, clip_other, w_time, w_out, wo_other),
        [((places, C), F32), ((C, half), BF16)],
        [pltpu.VMEM((places, C), BF16)],
        flops=MIDDLE,
    )
    (acc,) = call(
        functools.partial(first_kernel, frames),
        (acc, near, near_other, w_time),
        [((places, C), F32)],
        flops=FIRST,
    )
    (acc,) = call(
        functools.partial(second_kernel, frames), (acc, late, w_time), [((places, C), F32)], flops=SECOND
    )
    temporal, query = call(
        functools.partial(query_kernel, frames),
        (acc, late_other, w_time, wq, wq_other, norm_gain),
        [((places, half), BF16), ((C, places), BF16)],
        flops=QUERY,
    )
    count = width * frames * lax.axis_size("rows")
    (out,) = call(
        functools.partial(attend_kernel, [flip for _, flip in toks]),
        (*[part for part, _ in toks], query, temporal, wk, wk_other, wv, wv_other, wo),
        [((places, half), BF16)],
        [
            pltpu.VMEM((count, C), BF16),
            pltpu.VMEM((HEADS, count, 128), BF16),
            pltpu.VMEM((C, count), BF16),
            pltpu.VMEM((C, places), BF16),
        ],
        flops=ATTEND,
    )
    return out.reshape(clip_latent.shape)


def solution(mesh):
    return jax.shard_map(
        body,
        mesh=mesh,
        in_specs=(
            P(("groups", "frames"), "rows", None, "heads"),
            P(),
            P(),
            P(None, "heads"),
            P(None, "heads"),
            P(None, "heads"),
            P("heads", None),
            P(("groups", "frames", "rows"), "heads"),
        ),
        out_specs=P(("groups", "frames"), "rows", None, "heads"),
        check_vma=False,
    )
```

```python
import functools

import jax
import jax.numpy as jnp
from jax import lax
from jax.experimental import pallas as pl
from jax.experimental.pallas import tpu as pltpu
from jax.sharding import PartitionSpec as P

C = 640
HEADS = 8
EPS = 1e-05

LOAD, JOIN = 10**9, 10**9
MIDDLE, FIRST, SELECT, QUERY, ATTEND = 5 * 10**8, 5 * 10**8, 10**8, 10**9, 2 * 10**9
REST = 5 * 10**9
LATE = 1

F32 = jnp.float32
BF16 = jnp.bfloat16


def nt_dot(a, b):
    return lax.dot_general(a, b, (((1,), (1,)), ((), ())), preferred_element_type=F32)


def tn_dot(a, b):
    return lax.dot_general(a, b, (((0,), (0,)), ((), ())), preferred_element_type=F32)


def sibling(x):
    return lax.ppermute(x, "heads", [(0, 1), (1, 0)])


def swap(x, partner):
    frames, rows = lax.axis_size("frames"), lax.axis_size("rows")
    perm = []
    for frame in range(frames):
        for row in range(rows):
            for core in range(2):
                to = partner(frame, row, core)
                if to is not None:
                    perm.append((((frame * rows) + row) * 2 + core, ((to[0] * rows) + to[1]) * 2 + to[2]))
    return lax.ppermute(x, ("frames", "rows", "heads"), perm)


def swap_near(x):
    frames, rows = lax.axis_size("frames"), lax.axis_size("rows")

    def partner(frame, row, core):
        to = frame + 1 if frame % 2 == core else frame - 1
        if 0 <= to < frames:
            return to, row, core
        return (frame, row ^ 1, core) if rows % 2 == 0 else None

    return swap(x, partner)


def swap_bit(x, axis, bit):
    return lax.ppermute(x, axis, [(i, i ^ bit) for i in range(lax.axis_size(axis))])


VMEM = pl.BlockSpec(memory_space=pltpu.VMEM)


def call(kernel, operands, outs, scratch=(), flops=0):
    return pl.pallas_call(
        kernel,
        out_shape=[jax.ShapeDtypeStruct(shape, dtype) for shape, dtype in outs],
        in_specs=[VMEM] * len(operands),
        out_specs=[VMEM] * len(outs),
        scratch_shapes=list(scratch),
        compiler_params=pltpu.CompilerParams(vmem_limit_bytes=40 * 2**20),
        cost_estimate=pl.CostEstimate(flops=flops, bytes_accessed=0, transcendentals=0),
    )(*operands)


def stack_kernel(*refs):
    at = 0
    for ref in refs[:-1]:
        refs[-1][at : at + ref.shape[0]] = ref[...]
        at += ref.shape[0]


def load_kernel(*refs):
    count = len(refs) // 2
    for source, target in zip(refs[:count], refs[count:]):
        target[...] = source[...]


def load(*operands):
    return call(load_kernel, operands, [(x.shape, x.dtype) for x in operands], flops=LOAD)


def join_kernel(clip_ref, clip_other_ref, tok_ref, tok_other_ref, out_ref, own_ref):
    core = lax.axis_index("heads")
    places, half = clip_ref.shape
    for own, other, rows in ((clip_ref, clip_other_ref, slice(0, places)), (tok_ref, tok_other_ref, slice(places, None))):
        own, other = own[...], other[...]
        out_ref[rows, :half] = jnp.where(core == 0, own, other)
        out_ref[rows, half:] = jnp.where(core == 0, other, own)
    own_ref[...] = out_ref[places:]


def gather_tokens(own, near, near_other):
    frames, rows = lax.axis_size("frames"), lax.axis_size("rows")
    if frames == 4 and rows == 2:
        edge = lambda frame: frame in (0, frames - 1)
        far = swap(own, lambda f, r, c: (f ^ 2, r, c) if c == 0 else (f ^ 3, r, c) if edge(f) else (f, r ^ 1, c))
        across = swap(own, lambda f, r, c: (f ^ (2 if c else 1), r ^ 1, c))
        last = swap(own, lambda f, r, c: (f ^ 3, r ^ 1, c) if edge(f) == (c == 0) else (f, r ^ 1, c))
        shape = (3 * own.shape[0], C)
        (rest,) = call(stack_kernel, (far, across, last), [(shape, BF16)], flops=REST)
        return [(own, "all"), (near, "below"), (near_other, "below"), (rest, "inner"), (sibling(rest), "outer")]
    parts = [own]
    for axis, count in (("frames", frames), ("rows", rows)):
        assert count & (count - 1) == 0
        bit = 1
        while bit < count:
            held = parts[0]
            if len(parts) > 1:
                shape = (2 * held.shape[0], C)
                (held,) = call(stack_kernel, parts, [(shape, BF16)], flops=JOIN)
            parts = [held, swap_bit(held, axis, bit)]
            bit *= 2
    return [(part, "all") for part in parts]


def beside(near_ref, places, core, frames):
    frame = lax.axis_index("frames")
    after = lax.rem(frame, 2) == core
    there = jnp.where(after, frame < frames - 1, frame > 0)
    near = near_ref[:places]
    return jnp.where(there, near, jnp.zeros_like(near)), jnp.where(after, 2, 0)


def middle_kernel(full_ref, w_ref, acc_ref):
    full = full_ref[: acc_ref.shape[0]]
    acc_ref[...] = full.astype(F32) + jnp.dot(full, w_ref[1], preferred_element_type=F32)


def select_kernel(own_ref, other_ref, out_ref):
    core = lax.axis_index("heads")
    half = own_ref.shape[0]
    out_ref[:half] = jnp.where(core == 0, own_ref[:, :half], own_ref[:, half:])
    out_ref[half:] = jnp.where(core == 0, other_ref[:, :half], other_ref[:, half:])


def first_kernel(frames, acc_ref, near_ref, w_ref, sum_ref):
    near, tap = beside(near_ref, acc_ref.shape[0], lax.axis_index("heads"), frames)
    sum_ref[...] = acc_ref[...] + jnp.dot(near, w_ref[tap], preferred_element_type=F32)


def query_kernel(frames, acc_ref, near_ref, w_ref, wq_own_ref, wq_other_ref, gain_ref, temporal_ref, query_ref):
    core = lax.axis_index("heads")
    half = wq_own_ref.shape[0]
    near, tap = beside(near_ref, acc_ref.shape[0], 1 - core, frames)
    temporal = (acc_ref[...] + jnp.dot(near, w_ref[tap], preferred_element_type=F32)).astype(BF16)
    temporal_ref[...] = jnp.where(core == 0, temporal[:, :half], temporal[:, half:])
    feats = temporal.astype(F32)
    centre = jnp.mean(feats, axis=-1, keepdims=True)
    centred = feats - centre
    spread = jnp.mean(centred * centred, axis=-1, keepdims=True)
    normed = (centred * lax.rsqrt(spread + EPS) * gain_ref[...]).astype(BF16)
    scale = (C // HEADS) ** -0.5
    query_ref[:half] = (nt_dot(wq_own_ref[...], normed) * scale).astype(BF16)
    query_ref[half:] = (nt_dot(wq_other_ref[...], normed) * scale).astype(BF16)


def attend_kernel(uses, frames, *refs):
    core = lax.axis_index("heads")
    frame = lax.axis_index("frames")
    blocks, refs = refs[: len(uses)], refs[len(uses) :]
    query_ref, temporal_ref, wk_own_ref, wk_other_ref, wv_own_ref, wv_other_ref, wo_ref = refs[:7]
    out_ref, tokens, keys, values, attended = refs[7:]
    half = wk_own_ref.shape[0]
    size = C // HEADS
    inner = ((frame == 0) | (frame == frames - 1)) == (core == 0)
    at = 0
    for i, use in enumerate(uses):
        found = blocks[i][...]
        if use == "below":
            found = blocks[i][temporal_ref.shape[0] :]
        if use == "inner":
            last = found.shape[0] // 3 * 2
            tokens[at : at + found.shape[0] - last] = jnp.where(inner, found[last:], blocks[i + 1][last:])
            at += found.shape[0] - last
        if use in ("inner", "outer"):
            found = found[:last]
        tokens[at : at + found.shape[0]] = found
        at += found.shape[0]
    toks = tokens[...]
    for part, (wk_ref, wv_ref) in enumerate(((wk_own_ref, wv_own_ref), (wk_other_ref, wv_other_ref))):
        values[part * half : (part + 1) * half] = nt_dot(wv_ref[...], toks).astype(BF16)
        found = nt_dot(toks, wk_ref[...]).astype(BF16)
        for head in range(half // size):
            keys[part * (half // size) + head, :, :size] = found[:, head * size : (head + 1) * size]
    probs = []
    for head in range(HEADS):
        rows = slice(head * size, (head + 1) * size)
        scores = jnp.dot(keys[head, :, :size], query_ref[rows], preferred_element_type=F32)
        expo = jnp.exp(scores - jnp.max(scores, axis=0, keepdims=True))
        probs.append((expo.astype(BF16), 1.0 / jnp.sum(expo, axis=0, keepdims=True)))
    for head in range(HEADS):
        rows = slice(head * size, (head + 1) * size)
        prob, inverse = probs[head]
        mixed = jnp.dot(values[rows], prob, preferred_element_type=F32)
        attended[rows] = (mixed * inverse).astype(BF16)
    mixed = tn_dot(attended[...], wo_ref[...])
    out_ref[...] = (temporal_ref[...].astype(F32) + mixed).astype(BF16)


def body(clip_latent, norm_gain, w_time, w_query, w_key, w_value, w_out, reference_tokens):
    frames_here, rows_here, cols_here, half = clip_latent.shape
    assert frames_here == 1 and lax.axis_size("heads") == 2
    places = rows_here * cols_here
    width = reference_tokens.shape[0]
    clip = clip_latent.reshape(places, half)
    frames = lax.axis_size("frames")
    frames = lax.axis_size("frames")
    clip_other, toks_other = sibling(clip), sibling(reference_tokens)
    clip, toks = load(clip, reference_tokens)
    full, own = call(
        join_kernel,
        (clip, clip_other, toks, toks_other),
        [((places + width, C), BF16), ((width, C), BF16)],
        flops=JOIN,
    )
    near = swap_near(full)
    near_other = sibling(near)
    toks = gather_tokens(own, near, near_other)
    *wide, _ = lax.optimization_barrier((w_query.T, w_key.T, w_value.T, w_out, near if LATE else own))
    wq_other, wk_other, wv_other, wo_other = (sibling(x) for x in wide)
    wq, wk, wv = w_query.T, w_key.T, w_value.T
    (wo,) = call(select_kernel, (w_out, wo_other), [((C, half), BF16)], flops=SELECT)
    (acc,) = call(middle_kernel, (full, w_time), [((places, C), F32)], flops=MIDDLE)
    (acc,) = call(
        functools.partial(first_kernel, frames), (acc, near, w_time), [((places, C), F32)], flops=FIRST
    )
    temporal, query = call(
        functools.partial(query_kernel, frames),
        (acc, near_other, w_time, wq, wq_other, norm_gain),
        [((places, half), BF16), ((C, places), BF16)],
        flops=QUERY,
    )
    count = width * frames * lax.axis_size("rows")
    (out,) = call(
        functools.partial(attend_kernel, [use for _, use in toks], frames),
        (*[x for x, _ in toks], query, temporal, wk, wk_other, wv, wv_other, wo),
        [((places, half), BF16)],
        [
            pltpu.VMEM((count, C), BF16),
            pltpu.VMEM((HEADS, count, 128), BF16),
            pltpu.VMEM((C, count), BF16),
            pltpu.VMEM((C, places), BF16),
        ],
        flops=ATTEND,
    )
    return out.reshape(clip_latent.shape)


def solution(mesh):
    return jax.shard_map(
        body,
        mesh=mesh,
        in_specs=(
            P(("groups", "frames"), "rows", None, "heads"),
            P(),
            P(),
            P(None, "heads"),
            P(None, "heads"),
            P(None, "heads"),
            P("heads", None),
            P(("groups", "frames", "rows"), "heads"),
        ),
        out_specs=P(("groups", "frames"), "rows", None, "heads"),
        check_vma=False,
    )
```

```python
import functools

import jax
import jax.numpy as jnp
from jax import lax
from jax.experimental import pallas as pl
from jax.experimental.pallas import tpu as pltpu
from jax.sharding import PartitionSpec as P

C = 640
HEADS = 8
EPS = 1e-05

JOIN = 10 * 10**9
MIDDLE = 5 * 10**8
FIRST = 5 * 10**8
QUERY = 10**9
ATTEND = 2 * 10**9
WEIGHTS = 10**8
REST = 30 * 10**9

F32 = jnp.float32
BF16 = jnp.bfloat16


def nt_dot(a, b):
    return lax.dot_general(a, b, (((1,), (1,)), ((), ())), preferred_element_type=F32)


def tn_dot(a, b):
    return lax.dot_general(a, b, (((0,), (0,)), ((), ())), preferred_element_type=F32)


def sibling(x):
    return lax.ppermute(x, "heads", [(0, 1), (1, 0)])


def swap(x, partner):
    frames, rows = lax.axis_size("frames"), lax.axis_size("rows")
    perm = []
    for frame in range(frames):
        for row in range(rows):
            for core in range(2):
                to = partner(frame, row, core)
                if to is not None:
                    perm.append((((frame * rows) + row) * 2 + core, ((to[0] * rows) + to[1]) * 2 + to[2]))
    return lax.ppermute(x, ("frames", "rows", "heads"), perm)


def swap_frames(x, parity):
    frames, rows = lax.axis_size("frames"), lax.axis_size("rows")

    def partner(frame, row, core):
        to = frame + 1 if frame % 2 == parity else frame - 1
        if 0 <= to < frames:
            return to, row, core
        return (frame, row ^ 1, core) if rows % 2 == 0 else None

    return swap(x, partner)


def swap_bit(x, axis, bit):
    return lax.ppermute(x, axis, [(i, i ^ bit) for i in range(lax.axis_size(axis))])


VMEM = pl.BlockSpec(memory_space=pltpu.VMEM)


def call(kernel, operands, outs, scratch=(), flops=0):
    return pl.pallas_call(
        kernel,
        out_shape=[jax.ShapeDtypeStruct(shape, dtype) for shape, dtype in outs],
        in_specs=[VMEM] * len(operands),
        out_specs=[VMEM] * len(outs),
        scratch_shapes=list(scratch),
        compiler_params=pltpu.CompilerParams(vmem_limit_bytes=40 * 2**20),
        cost_estimate=pl.CostEstimate(flops=flops, bytes_accessed=0, transcendentals=0),
    )(*operands)


def stack_kernel(*refs):
    at = 0
    for ref in refs[:-1]:
        refs[-1][at : at + ref.shape[0]] = ref[...]
        at += ref.shape[0]


def join_kernel(own_ref, other_ref, out_ref):
    core = lax.axis_index("heads")
    half = own_ref.shape[1]
    own, other = own_ref[...], other_ref[...]
    out_ref[:, :half] = jnp.where(core == 0, own, other)
    out_ref[:, half:] = jnp.where(core == 0, other, own)


def gather_tokens(own):
    frames, rows = lax.axis_size("frames"), lax.axis_size("rows")
    if frames == 4 and rows == 2:
        far = [swap(own, lambda f, r, c, d=d: (f ^ d, r ^ c, c)) for d in (3, 2, 1)]
        (rest,) = call(stack_kernel, far, [((3 * own.shape[0], C), BF16)], flops=REST)
        return [own, swap_bit(own, "rows", 1)], [rest]
    parts = [own]
    for axis, count in (("frames", frames), ("rows", rows)):
        assert count & (count - 1) == 0
        bit = 1
        while bit < count:
            held = parts[0]
            if len(parts) > 1:
                shape = (2 * held.shape[0], C)
                (held,) = call(stack_kernel, parts, [(shape, BF16)], flops=JOIN)
            parts = [held, swap_bit(held, axis, bit)]
            bit *= 2
    return parts, []


def halves(core, half):
    own = pl.multiple_of(core * half, 16)
    return pl.ds(own, half), pl.ds(pl.multiple_of(half - own, 16), half)


def beside(refs, w_ref, channels, frames):
    frame = lax.axis_index("frames")
    terms = None
    for parity, ref in enumerate(refs):
        after = lax.rem(frame, 2) == parity
        there = jnp.where(after, frame < frames - 1, frame > 0)
        near = ref[...]
        near = jnp.where(there, near, jnp.zeros_like(near))
        term = jnp.dot(near, w_ref[jnp.where(after, 2, 0), channels], preferred_element_type=F32)
        terms = term if terms is None else terms + term
    return terms


def middle_kernel(own_ref, other_ref, w_ref, acc_ref, full):
    join_kernel(own_ref, other_ref, full)
    whole = full[...]
    acc_ref[...] = whole.astype(F32) + jnp.dot(whole, w_ref[1], preferred_element_type=F32)


def weights_kernel(*refs):
    for i, ref in enumerate(refs[:-1]):
        refs[-1][i] = ref[...]


def first_kernel(frames, acc_ref, even_ref, odd_ref, w_ref, sum_ref):
    own = halves(lax.axis_index("heads"), even_ref.shape[1])[0]
    sum_ref[...] = acc_ref[...] + beside((even_ref, odd_ref), w_ref, own, frames)


def query_kernel(frames, acc_ref, even_ref, odd_ref, w_ref, held_ref, met_ref, gain_ref, temporal_ref, query_ref):
    core = lax.axis_index("heads")
    half = held_ref.shape[1]
    other = halves(core, half)[1]
    temporal = (acc_ref[...] + beside((even_ref, odd_ref), w_ref, other, frames)).astype(BF16)
    temporal_ref[...] = jnp.where(core == 0, temporal[:, :half], temporal[:, half:])
    feats = temporal.astype(F32)
    centre = jnp.mean(feats, axis=-1, keepdims=True)
    centred = feats - centre
    spread = jnp.mean(centred * centred, axis=-1, keepdims=True)
    normed = (centred * lax.rsqrt(spread + EPS) * gain_ref[...]).astype(BF16)
    scale = (C // HEADS) ** -0.5
    query_ref[:half] = (nt_dot(held_ref[0], normed) * scale).astype(BF16)
    query_ref[half:] = (nt_dot(met_ref[0], normed) * scale).astype(BF16)


def attend_kernel(parts, *refs):
    core = lax.axis_index("heads")
    blocks, refs = refs[:parts], refs[parts:]
    query_ref, temporal_ref, held_ref, met_ref, out_ref, tokens, keys, values, attended, out_weights = refs
    half = held_ref.shape[1]
    size = C // HEADS
    at = 0
    for ref in blocks:
        tokens[at : at + ref.shape[0]] = ref[...]
        at += ref.shape[0]
    toks = tokens[...]
    for part, w_ref in enumerate((held_ref, met_ref)):
        out_weights[part * half : (part + 1) * half] = jnp.where(core == 0, w_ref[3, :, :half], w_ref[3, :, half:])
        values[part * half : (part + 1) * half] = nt_dot(w_ref[2], toks).astype(BF16)
        found = nt_dot(toks, w_ref[1]).astype(BF16)
        for head in range(half // size):
            keys[part * (half // size) + head, :, :size] = found[:, head * size : (head + 1) * size]
    probs = []
    for head in range(HEADS):
        rows = slice(head * size, (head + 1) * size)
        scores = jnp.dot(keys[head, :, :size], query_ref[rows], preferred_element_type=F32)
        expo = jnp.exp(scores - jnp.max(scores, axis=0, keepdims=True))
        probs.append((expo.astype(BF16), 1.0 / jnp.sum(expo, axis=0, keepdims=True)))
    for head in range(HEADS):
        rows = slice(head * size, (head + 1) * size)
        prob, inverse = probs[head]
        mixed = jnp.dot(values[rows], prob, preferred_element_type=F32)
        attended[rows] = (mixed * inverse).astype(BF16)
    mixed = tn_dot(attended[...], out_weights[...])
    out_ref[...] = (temporal_ref[...].astype(F32) + mixed).astype(BF16)


def body(clip_latent, norm_gain, w_time, w_query, w_key, w_value, w_out, reference_tokens):
    frames_here, rows_here, cols_here, half = clip_latent.shape
    assert frames_here == 1 and lax.axis_size("heads") == 2
    places = rows_here * cols_here
    width = reference_tokens.shape[0]
    clip = clip_latent.reshape(places, half)
    frames = lax.axis_size("frames")
    frames = lax.axis_size("frames")
    clip_other, toks_other = sibling(clip), sibling(reference_tokens)
    clip_other, toks_other = lax.optimization_barrier((clip_other, toks_other))
    even, odd = swap_frames(clip, 0), swap_frames(clip, 1)
    even_other, odd_other = sibling(even), sibling(odd)
    (own,) = call(join_kernel, (reference_tokens, toks_other), [((width, C), BF16)], flops=JOIN)
    toks, rest = gather_tokens(own)
    (acc,) = call(
        middle_kernel,
        (clip, clip_other, w_time),
        [((places, C), F32)],
        [pltpu.VMEM((places, C), BF16)],
        flops=MIDDLE,
    )
    *wide, _ = lax.optimization_barrier((w_query.T, w_key.T, w_value.T, w_out, acc))
    (held,) = call(weights_kernel, wide, [((4,) + w_out.shape, BF16)], flops=WEIGHTS)
    met = sibling(held)
    (acc,) = call(
        functools.partial(first_kernel, frames), (acc, even, odd, w_time), [((places, C), F32)], flops=FIRST
    )
    temporal, query = call(
        functools.partial(query_kernel, frames),
        (acc, even_other, odd_other, w_time, held, met, norm_gain),
        [((places, half), BF16), ((C, places), BF16)],
        flops=QUERY,
    )
    for part in rest:
        toks += [part, sibling(part)]
    count = width * frames * lax.axis_size("rows")
    (out,) = call(
        functools.partial(attend_kernel, len(toks)),
        (*toks, query, temporal, held, met),
        [((places, half), BF16)],
        [
            pltpu.VMEM((count, C), BF16),
            pltpu.VMEM((HEADS, count, 128), BF16),
            pltpu.VMEM((C, count), BF16),
            pltpu.VMEM((C, places), BF16),
            pltpu.VMEM((C, half), BF16),
        ],
        flops=ATTEND,
    )
    return out.reshape(clip_latent.shape)


def solution(mesh):
    return jax.shard_map(
        body,
        mesh=mesh,
        in_specs=(
            P(("groups", "frames"), "rows", None, "heads"),
            P(),
            P(),
            P(None, "heads"),
            P(None, "heads"),
            P(None, "heads"),
            P("heads", None),
            P(("groups", "frames", "rows"), "heads"),
        ),
        out_specs=P(("groups", "frames"), "rows", None, "heads"),
        check_vma=False,
    )
```

```python
import functools

import jax
import jax.numpy as jnp
from jax import lax
from jax.experimental import pallas as pl
from jax.experimental.pallas import tpu as pltpu
from jax.sharding import PartitionSpec as P

C = 640
HEADS = 8
EPS = 1e-05
LANES = 128

JOIN = 10 * 10**9
AHEAD = 20 * 10**9
MIDDLE = 5 * 10**8
FIRST = 5 * 10**8
QUERY = 10**9
ATTEND = 2 * 10**9
WEIGHTS = 10**8
REST = 30 * 10**9

F32 = jnp.float32
BF16 = jnp.bfloat16


def nt_dot(a, b):
    return lax.dot_general(a, b, (((1,), (1,)), ((), ())), preferred_element_type=F32)


def tn_dot(a, b):
    return lax.dot_general(a, b, (((0,), (0,)), ((), ())), preferred_element_type=F32)


def sibling(x):
    return lax.ppermute(x, "heads", [(0, 1), (1, 0)])


def swap(x, partner):
    frames, rows = lax.axis_size("frames"), lax.axis_size("rows")
    perm = []
    for frame in range(frames):
        for row in range(rows):
            for core in range(2):
                to = partner(frame, row, core)
                if to is not None:
                    perm.append((((frame * rows) + row) * 2 + core, ((to[0] * rows) + to[1]) * 2 + to[2]))
    return lax.ppermute(x, ("frames", "rows", "heads"), perm)


def swap_frames(x, parity):
    frames, rows = lax.axis_size("frames"), lax.axis_size("rows")

    def partner(frame, row, core):
        to = frame + 1 if frame % 2 == parity else frame - 1
        if 0 <= to < frames:
            return to, row, core
        return (frame, row ^ 1, core) if rows % 2 == 0 else None

    return swap(x, partner)


def swap_bit(x, axis, bit):
    return lax.ppermute(x, axis, [(i, i ^ bit) for i in range(lax.axis_size(axis))])


VMEM = pl.BlockSpec(memory_space=pltpu.VMEM)


def call(kernel, operands, outs, scratch=(), flops=0):
    return pl.pallas_call(
        kernel,
        out_shape=[jax.ShapeDtypeStruct(shape, dtype) for shape, dtype in outs],
        in_specs=[VMEM] * len(operands),
        out_specs=[VMEM] * len(outs),
        scratch_shapes=list(scratch),
        compiler_params=pltpu.CompilerParams(vmem_limit_bytes=40 * 2**20),
        cost_estimate=pl.CostEstimate(flops=flops, bytes_accessed=0, transcendentals=0),
    )(*operands)


def stack_kernel(*refs):
    at = 0
    for ref in refs[:-1]:
        refs[-1][at : at + ref.shape[0]] = ref[...]
        at += ref.shape[0]


def join_kernel(own_ref, other_ref, out_ref):
    core = lax.axis_index("heads")
    half = own_ref.shape[1]
    own, other = own_ref[...], other_ref[...]
    out_ref[:, :half] = jnp.where(core == 0, own, other)
    out_ref[:, half:] = jnp.where(core == 0, other, own)


def blank_kernel(_, out_ref):
    out_ref[...] = jnp.zeros_like(out_ref)


def first_join_kernel(own_ref, other_ref, _, out_ref, packed_ref):
    join_kernel(own_ref, other_ref, out_ref)
    width = out_ref.shape[0]
    for i in range(C // LANES):
        packed_ref[i * width : (i + 1) * width] = out_ref[:, i * LANES : (i + 1) * LANES]


def unpack_kernel(*refs):
    out_ref = refs[-1]
    width = refs[0].shape[0] * LANES // C
    for at, ref in enumerate(refs[:-1]):
        for i in range(C // LANES):
            out_ref[at * width : (at + 1) * width, i * LANES : (i + 1) * LANES] = ref[i * width : (i + 1) * width]


def gather_tokens(own, packed):
    frames, rows = lax.axis_size("frames"), lax.axis_size("rows")
    if frames == 4 and rows == 2:
        far = [swap(packed, lambda f, r, c, d=d: (f ^ d, r ^ c, c)) for d in (3, 2, 1)]
        (rest,) = call(unpack_kernel, far, [((3 * own.shape[0], C), BF16)], flops=REST)
        return [own, swap_bit(own, "rows", 1)], [rest]
    parts = [own]
    for axis, count in (("frames", frames), ("rows", rows)):
        assert count & (count - 1) == 0
        bit = 1
        while bit < count:
            held = parts[0]
            if len(parts) > 1:
                shape = (2 * held.shape[0], C)
                (held,) = call(stack_kernel, parts, [(shape, BF16)], flops=JOIN)
            parts = [held, swap_bit(held, axis, bit)]
            bit *= 2
    return parts, []


def halves(core, half):
    own = pl.multiple_of(core * half, 16)
    return pl.ds(own, half), pl.ds(pl.multiple_of(half - own, 16), half)


def beside(refs, w_ref, channels, frames):
    frame = lax.axis_index("frames")
    terms = None
    for parity, ref in enumerate(refs):
        after = lax.rem(frame, 2) == parity
        there = jnp.where(after, frame < frames - 1, frame > 0)
        near = ref[...]
        near = jnp.where(there, near, jnp.zeros_like(near))
        term = jnp.dot(near, w_ref[jnp.where(after, 2, 0), channels], preferred_element_type=F32)
        terms = term if terms is None else terms + term
    return terms


def middle_kernel(own_ref, other_ref, w_ref, acc_ref, full):
    join_kernel(own_ref, other_ref, full)
    whole = full[...]
    acc_ref[...] = whole.astype(F32) + jnp.dot(whole, w_ref[1], preferred_element_type=F32)


def weights_kernel(wq_ref, wk_ref, wv_ref, wo_ref, held_ref, out_ref):
    core = lax.axis_index("heads")
    half = wo_ref.shape[0]
    for i, ref in enumerate((wq_ref, wk_ref, wv_ref)):
        held_ref[i * half : (i + 1) * half] = ref[...]
    left, right = wo_ref[:, :half], wo_ref[:, half:]
    out_ref[...] = jnp.where(core == 0, left, right)
    sent = jnp.where(core == 0, right, left)
    held_ref[3 * half :, :half] = sent[: half // 2]
    held_ref[3 * half :, half:] = sent[half // 2 :]


def first_kernel(frames, acc_ref, even_ref, odd_ref, w_ref, sum_ref):
    own = halves(lax.axis_index("heads"), even_ref.shape[1])[0]
    sum_ref[...] = acc_ref[...] + beside((even_ref, odd_ref), w_ref, own, frames)


def query_kernel(frames, acc_ref, even_ref, odd_ref, w_ref, held_ref, met_ref, gain_ref, temporal_ref, query_ref):
    core = lax.axis_index("heads")
    half = held_ref.shape[1] // 2
    other = halves(core, half)[1]
    temporal = (acc_ref[...] + beside((even_ref, odd_ref), w_ref, other, frames)).astype(BF16)
    temporal_ref[...] = jnp.where(core == 0, temporal[:, :half], temporal[:, half:])
    feats = temporal.astype(F32)
    centre = jnp.mean(feats, axis=-1, keepdims=True)
    centred = feats - centre
    spread = jnp.mean(centred * centred, axis=-1, keepdims=True)
    normed = (centred * lax.rsqrt(spread + EPS) * gain_ref[...]).astype(BF16)
    scale = (C // HEADS) ** -0.5
    query_ref[:half] = (nt_dot(held_ref[:half], normed) * scale).astype(BF16)
    query_ref[half:] = (nt_dot(met_ref[:half], normed) * scale).astype(BF16)


def attend_kernel(parts, *refs):
    blocks, refs = refs[:parts], refs[parts:]
    query_ref, temporal_ref, held_ref, met_ref, wo_ref, out_ref, tokens, keys, values, attended, out_weights = refs
    half = held_ref.shape[1] // 2
    size = C // HEADS
    at = 0
    for ref in blocks:
        tokens[at : at + ref.shape[0]] = ref[...]
        at += ref.shape[0]
    toks = tokens[...]
    wk, wv = (
        jnp.concatenate([ref[i * half : (i + 1) * half] for ref in (held_ref, met_ref)], axis=0) for i in (1, 2)
    )
    values[...] = nt_dot(wv, toks).astype(BF16)
    found = nt_dot(toks, wk).astype(BF16)
    for head in range(HEADS):
        keys[head, :, :size] = found[:, head * size : (head + 1) * size]
    probs = []
    for head in range(HEADS):
        rows = slice(head * size, (head + 1) * size)
        scores = jnp.dot(keys[head, :, :size], query_ref[rows], preferred_element_type=F32)
        expo = jnp.exp(scores - jnp.max(scores, axis=0, keepdims=True))
        probs.append((expo.astype(BF16), 1.0 / jnp.sum(expo, axis=0, keepdims=True)))
    for head in range(HEADS):
        rows = slice(head * size, (head + 1) * size)
        prob, inverse = probs[head]
        mixed = jnp.dot(values[rows], prob, preferred_element_type=F32)
        attended[rows] = (mixed * inverse).astype(BF16)
    out_weights[:half] = wo_ref[...]
    out_weights[half : half + half // 2] = met_ref[3 * half :, :half]
    out_weights[half + half // 2 :] = met_ref[3 * half :, half:]
    mixed = tn_dot(attended[...], out_weights[...])
    out_ref[...] = (temporal_ref[...].astype(F32) + mixed).astype(BF16)


def body(clip_latent, norm_gain, w_time, w_query, w_key, w_value, w_out, reference_tokens):
    frames_here, rows_here, cols_here, half = clip_latent.shape
    assert frames_here == 1 and lax.axis_size("heads") == 2
    places = rows_here * cols_here
    width = reference_tokens.shape[0]
    clip = clip_latent.reshape(places, half)
    frames = lax.axis_size("frames")
    frames = lax.axis_size("frames")
    clip_other, toks_other = sibling(clip), sibling(reference_tokens)
    clip_other, toks_other = lax.optimization_barrier((clip_other, toks_other))
    even, odd = swap_frames(clip, 0), swap_frames(clip, 1)
    even_other, odd_other = sibling(even), sibling(odd)
    (blank,) = call(blank_kernel, (toks_other,), [((8, 128), F32)], flops=AHEAD)
    own, packed = call(
        first_join_kernel,
        (reference_tokens, toks_other, blank),
        [((width, C), BF16), ((width * C // LANES, LANES), BF16)],
        flops=JOIN,
    )
    toks, rest = gather_tokens(own, packed)
    (acc,) = call(
        middle_kernel,
        (clip, clip_other, w_time),
        [((places, C), F32)],
        [pltpu.VMEM((places, C), BF16)],
        flops=MIDDLE,
    )
    *wide, _ = lax.optimization_barrier((w_query.T, w_key.T, w_value.T, w_out, acc))
    held, wo = call(weights_kernel, wide, [((7 * half // 2, C), BF16), ((half, half), BF16)], flops=WEIGHTS)
    met = sibling(held)
    (acc,) = call(
        functools.partial(first_kernel, frames), (acc, even, odd, w_time), [((places, C), F32)], flops=FIRST
    )
    temporal, query = call(
        functools.partial(query_kernel, frames),
        (acc, even_other, odd_other, w_time, held, met, norm_gain),
        [((places, half), BF16), ((C, places), BF16)],
        flops=QUERY,
    )
    for part in rest:
        toks += [part, sibling(part)]
    count = width * frames * lax.axis_size("rows")
    (out,) = call(
        functools.partial(attend_kernel, len(toks)),
        (*toks, query, temporal, held, met, wo),
        [((places, half), BF16)],
        [
            pltpu.VMEM((count, C), BF16),
            pltpu.VMEM((HEADS, count, 128), BF16),
            pltpu.VMEM((C, count), BF16),
            pltpu.VMEM((C, places), BF16),
            pltpu.VMEM((C, half), BF16),
        ],
        flops=ATTEND,
    )
    return out.reshape(clip_latent.shape)


def solution(mesh):
    return jax.shard_map(
        body,
        mesh=mesh,
        in_specs=(
            P(("groups", "frames"), "rows", None, "heads"),
            P(),
            P(),
            P(None, "heads"),
            P(None, "heads"),
            P(None, "heads"),
            P("heads", None),
            P(("groups", "frames", "rows"), "heads"),
        ),
        out_specs=P(("groups", "frames"), "rows", None, "heads"),
        check_vma=False,
    )
```

```python
import functools

import jax
import jax.numpy as jnp
from jax import lax
from jax.experimental import pallas as pl
from jax.experimental.pallas import tpu as pltpu
from jax.sharding import PartitionSpec as P

C = 640
HEADS = 8
EPS = 1e-05
LANES = 128

JOIN = 10 * 10**9
AHEAD = 20 * 10**9
MIDDLE = 5 * 10**8
FIRST = 5 * 10**8
QUERY = 10**9
ATTEND = 2 * 10**9
WEIGHTS = 10**8
REST = 30 * 10**9

F32 = jnp.float32
BF16 = jnp.bfloat16


def nt_dot(a, b):
    return lax.dot_general(a, b, (((1,), (1,)), ((), ())), preferred_element_type=F32)


def tn_dot(a, b):
    return lax.dot_general(a, b, (((0,), (0,)), ((), ())), preferred_element_type=F32)


def sibling(x):
    return lax.ppermute(x, "heads", [(0, 1), (1, 0)])


def swap(x, partner):
    frames, rows = lax.axis_size("frames"), lax.axis_size("rows")
    perm = []
    for frame in range(frames):
        for row in range(rows):
            for core in range(2):
                to = partner(frame, row, core)
                if to is not None:
                    perm.append((((frame * rows) + row) * 2 + core, ((to[0] * rows) + to[1]) * 2 + to[2]))
    return lax.ppermute(x, ("frames", "rows", "heads"), perm)


def swap_frames(x, parity):
    frames, rows = lax.axis_size("frames"), lax.axis_size("rows")

    def partner(frame, row, core):
        to = frame + 1 if frame % 2 == parity else frame - 1
        if 0 <= to < frames:
            return to, row, core
        return (frame, row ^ 1, core) if rows % 2 == 0 else None

    return swap(x, partner)


def swap_bit(x, axis, bit):
    return lax.ppermute(x, axis, [(i, i ^ bit) for i in range(lax.axis_size(axis))])


VMEM = pl.BlockSpec(memory_space=pltpu.VMEM)


def call(kernel, operands, outs, scratch=(), flops=0):
    return pl.pallas_call(
        kernel,
        out_shape=[jax.ShapeDtypeStruct(shape, dtype) for shape, dtype in outs],
        in_specs=[VMEM] * len(operands),
        out_specs=[VMEM] * len(outs),
        scratch_shapes=list(scratch),
        compiler_params=pltpu.CompilerParams(vmem_limit_bytes=40 * 2**20),
        cost_estimate=pl.CostEstimate(flops=flops, bytes_accessed=0, transcendentals=0),
    )(*operands)


def stack_kernel(*refs):
    at = 0
    for ref in refs[:-1]:
        refs[-1][at : at + ref.shape[0]] = ref[...]
        at += ref.shape[0]


def join_kernel(own_ref, other_ref, out_ref):
    core = lax.axis_index("heads")
    half = own_ref.shape[1]
    own, other = own_ref[...], other_ref[...]
    out_ref[:, :half] = jnp.where(core == 0, own, other)
    out_ref[:, half:] = jnp.where(core == 0, other, own)


def blank_kernel(_, out_ref):
    out_ref[...] = jnp.zeros_like(out_ref)


def first_join_kernel(own_ref, other_ref, _, out_ref, packed_ref):
    join_kernel(own_ref, other_ref, out_ref)
    width = out_ref.shape[0]
    for i in range(C // LANES):
        packed_ref[i * width : (i + 1) * width] = out_ref[:, i * LANES : (i + 1) * LANES]


def unpack_kernel(*refs):
    out_ref = refs[-1]
    width = refs[0].shape[0] * LANES // C
    for at, ref in enumerate(refs[:-1]):
        for i in range(C // LANES):
            out_ref[at * width : (at + 1) * width, i * LANES : (i + 1) * LANES] = ref[i * width : (i + 1) * width]


def gather_tokens(own, packed):
    frames, rows = lax.axis_size("frames"), lax.axis_size("rows")
    if frames == 4 and rows == 2:
        far = [swap(packed, lambda f, r, c, d=d: (f ^ d, r ^ c, c)) for d in (2, 1, 3)]
        (rest,) = call(unpack_kernel, far, [((3 * own.shape[0], C), BF16)], flops=REST)
        return [own, swap_bit(own, "rows", 1)], [rest]
    parts = [own]
    for axis, count in (("frames", frames), ("rows", rows)):
        assert count & (count - 1) == 0
        bit = 1
        while bit < count:
            held = parts[0]
            if len(parts) > 1:
                shape = (2 * held.shape[0], C)
                (held,) = call(stack_kernel, parts, [(shape, BF16)], flops=JOIN)
            parts = [held, swap_bit(held, axis, bit)]
            bit *= 2
    return parts, []


def halves(core, half):
    own = pl.multiple_of(core * half, 16)
    return pl.ds(own, half), pl.ds(pl.multiple_of(half - own, 16), half)


def beside(refs, w_ref, channels, frames):
    frame = lax.axis_index("frames")
    terms = None
    for parity, ref in enumerate(refs):
        after = lax.rem(frame, 2) == parity
        there = jnp.where(after, frame < frames - 1, frame > 0)
        near = ref[...]
        near = jnp.where(there, near, jnp.zeros_like(near))
        term = jnp.dot(near, w_ref[jnp.where(after, 2, 0), channels], preferred_element_type=F32)
        terms = term if terms is None else terms + term
    return terms


def middle_kernel(own_ref, other_ref, w_ref, acc_ref, full):
    join_kernel(own_ref, other_ref, full)
    whole = full[...]
    acc_ref[...] = whole.astype(F32) + jnp.dot(whole, w_ref[1], preferred_element_type=F32)


def weights_kernel(wq_ref, wk_ref, wv_ref, wo_ref, held_ref, out_ref):
    core = lax.axis_index("heads")
    half = wo_ref.shape[0]
    for i, ref in enumerate((wq_ref, wk_ref, wv_ref)):
        held_ref[i * half : (i + 1) * half] = ref[...]
    left, right = wo_ref[:, :half], wo_ref[:, half:]
    out_ref[...] = jnp.where(core == 0, left, right)
    sent = jnp.where(core == 0, right, left)
    held_ref[3 * half :, :half] = sent[: half // 2]
    held_ref[3 * half :, half:] = sent[half // 2 :]


def first_kernel(frames, acc_ref, even_ref, odd_ref, w_ref, sum_ref):
    own = halves(lax.axis_index("heads"), even_ref.shape[1])[0]
    sum_ref[...] = acc_ref[...] + beside((even_ref, odd_ref), w_ref, own, frames)


def query_kernel(frames, acc_ref, even_ref, odd_ref, w_ref, held_ref, met_ref, gain_ref, temporal_ref, query_ref):
    core = lax.axis_index("heads")
    half = held_ref.shape[1] // 2
    other = halves(core, half)[1]
    temporal = (acc_ref[...] + beside((even_ref, odd_ref), w_ref, other, frames)).astype(BF16)
    temporal_ref[...] = jnp.where(core == 0, temporal[:, :half], temporal[:, half:])
    feats = temporal.astype(F32)
    centre = jnp.mean(feats, axis=-1, keepdims=True)
    centred = feats - centre
    spread = jnp.mean(centred * centred, axis=-1, keepdims=True)
    normed = (centred * lax.rsqrt(spread + EPS) * gain_ref[...]).astype(BF16)
    scale = (C // HEADS) ** -0.5
    query_ref[:half] = (nt_dot(held_ref[:half], normed) * scale).astype(BF16)
    query_ref[half:] = (nt_dot(met_ref[:half], normed) * scale).astype(BF16)


def attend_kernel(parts, *refs):
    blocks, refs = refs[:parts], refs[parts:]
    query_ref, temporal_ref, held_ref, met_ref, wo_ref, out_ref, tokens, keys, values, attended, out_weights = refs
    half = held_ref.shape[1] // 2
    size = C // HEADS
    at = 0
    for ref in blocks:
        tokens[at : at + ref.shape[0]] = ref[...]
        at += ref.shape[0]
    toks = tokens[...]
    wk, wv = (
        jnp.concatenate([ref[i * half : (i + 1) * half] for ref in (held_ref, met_ref)], axis=0) for i in (1, 2)
    )
    values[...] = nt_dot(wv, toks).astype(BF16)
    found = nt_dot(toks, wk).astype(BF16)
    for head in range(HEADS):
        keys[head, :, :size] = found[:, head * size : (head + 1) * size]
    probs = []
    for head in range(HEADS):
        rows = slice(head * size, (head + 1) * size)
        scores = jnp.dot(keys[head, :, :size], query_ref[rows], preferred_element_type=F32)
        expo = jnp.exp(scores - jnp.max(scores, axis=0, keepdims=True))
        probs.append((expo.astype(BF16), 1.0 / jnp.sum(expo, axis=0, keepdims=True)))
    for head in range(HEADS):
        rows = slice(head * size, (head + 1) * size)
        prob, inverse = probs[head]
        mixed = jnp.dot(values[rows], prob, preferred_element_type=F32)
        attended[rows] = (mixed * inverse).astype(BF16)
    out_weights[:half] = wo_ref[...]
    out_weights[half : half + half // 2] = met_ref[3 * half :, :half]
    out_weights[half + half // 2 :] = met_ref[3 * half :, half:]
    mixed = tn_dot(attended[...], out_weights[...])
    out_ref[...] = (temporal_ref[...].astype(F32) + mixed).astype(BF16)


def body(clip_latent, norm_gain, w_time, w_query, w_key, w_value, w_out, reference_tokens):
    frames_here, rows_here, cols_here, half = clip_latent.shape
    assert frames_here == 1 and lax.axis_size("heads") == 2
    places = rows_here * cols_here
    width = reference_tokens.shape[0]
    clip = clip_latent.reshape(places, half)
    frames = lax.axis_size("frames")
    frames = lax.axis_size("frames")
    clip_other, toks_other = sibling(clip), sibling(reference_tokens)
    clip_other, toks_other = lax.optimization_barrier((clip_other, toks_other))
    even, odd = swap_frames(clip, 0), swap_frames(clip, 1)
    even_other, odd_other = sibling(even), sibling(odd)
    (blank,) = call(blank_kernel, (toks_other,), [((8, 128), F32)], flops=AHEAD)
    own, packed = call(
        first_join_kernel,
        (reference_tokens, toks_other, blank),
        [((width, C), BF16), ((width * C // LANES, LANES), BF16)],
        flops=JOIN,
    )
    toks, rest = gather_tokens(own, packed)
    (acc,) = call(
        middle_kernel,
        (clip, clip_other, w_time),
        [((places, C), F32)],
        [pltpu.VMEM((places, C), BF16)],
        flops=MIDDLE,
    )
    *wide, _ = lax.optimization_barrier((w_query.T, w_key.T, w_value.T, w_out, acc))
    held, wo = call(weights_kernel, wide, [((7 * half // 2, C), BF16), ((half, half), BF16)], flops=WEIGHTS)
    met = sibling(held)
    (acc,) = call(
        functools.partial(first_kernel, frames), (acc, even, odd, w_time), [((places, C), F32)], flops=FIRST
    )
    temporal, query = call(
        functools.partial(query_kernel, frames),
        (acc, even_other, odd_other, w_time, held, met, norm_gain),
        [((places, half), BF16), ((C, places), BF16)],
        flops=QUERY,
    )
    for part in rest:
        toks += [part, sibling(part)]
    count = width * frames * lax.axis_size("rows")
    (out,) = call(
        functools.partial(attend_kernel, len(toks)),
        (*toks, query, temporal, held, met, wo),
        [((places, half), BF16)],
        [
            pltpu.VMEM((count, C), BF16),
            pltpu.VMEM((HEADS, count, 128), BF16),
            pltpu.VMEM((C, count), BF16),
            pltpu.VMEM((C, places), BF16),
            pltpu.VMEM((C, half), BF16),
        ],
        flops=ATTEND,
    )
    return out.reshape(clip_latent.shape)


def solution(mesh):
    return jax.shard_map(
        body,
        mesh=mesh,
        in_specs=(
            P(("groups", "frames"), "rows", None, "heads"),
            P(),
            P(),
            P(None, "heads"),
            P(None, "heads"),
            P(None, "heads"),
            P("heads", None),
            P(("groups", "frames", "rows"), "heads"),
        ),
        out_specs=P(("groups", "frames"), "rows", None, "heads"),
        check_vma=False,
    )
```

```python
import functools

import jax
import jax.numpy as jnp
from jax import lax
from jax.experimental import pallas as pl
from jax.experimental.pallas import tpu as pltpu
from jax.sharding import PartitionSpec as P

C = 640
HEADS = 8
EPS = 1e-05
LANES = 128

JOIN = 10 * 10**9
AHEAD = 20 * 10**9
MIDDLE = 5 * 10**8
FIRST = 5 * 10**8
QUERY = 10**9
ATTEND = 2 * 10**9
WEIGHTS = 10**8
REST = 30 * 10**9

F32 = jnp.float32
BF16 = jnp.bfloat16


def nt_dot(a, b):
    return lax.dot_general(a, b, (((1,), (1,)), ((), ())), preferred_element_type=F32)


def tn_dot(a, b):
    return lax.dot_general(a, b, (((0,), (0,)), ((), ())), preferred_element_type=F32)


def sibling(x):
    return lax.ppermute(x, "heads", [(0, 1), (1, 0)])


def swap(x, partner):
    frames, rows = lax.axis_size("frames"), lax.axis_size("rows")
    perm = []
    for frame in range(frames):
        for row in range(rows):
            for core in range(2):
                to = partner(frame, row, core)
                if to is not None:
                    perm.append((((frame * rows) + row) * 2 + core, ((to[0] * rows) + to[1]) * 2 + to[2]))
    return lax.ppermute(x, ("frames", "rows", "heads"), perm)


def swap_frames(x, parity):
    frames, rows = lax.axis_size("frames"), lax.axis_size("rows")

    def partner(frame, row, core):
        to = frame + 1 if frame % 2 == parity else frame - 1
        if 0 <= to < frames:
            return to, row, core
        return (frame, row ^ 1, core) if rows % 2 == 0 else None

    return swap(x, partner)


def swap_bit(x, axis, bit):
    return lax.ppermute(x, axis, [(i, i ^ bit) for i in range(lax.axis_size(axis))])


VMEM = pl.BlockSpec(memory_space=pltpu.VMEM)


def call(kernel, operands, outs, scratch=(), flops=0):
    return pl.pallas_call(
        kernel,
        out_shape=[jax.ShapeDtypeStruct(shape, dtype) for shape, dtype in outs],
        in_specs=[VMEM] * len(operands),
        out_specs=[VMEM] * len(outs),
        scratch_shapes=list(scratch),
        compiler_params=pltpu.CompilerParams(vmem_limit_bytes=40 * 2**20),
        cost_estimate=pl.CostEstimate(flops=flops, bytes_accessed=0, transcendentals=0),
    )(*operands)


def stack_kernel(*refs):
    at = 0
    for ref in refs[:-1]:
        refs[-1][at : at + ref.shape[0]] = ref[...]
        at += ref.shape[0]


def join_kernel(own_ref, other_ref, out_ref):
    core = lax.axis_index("heads")
    half = own_ref.shape[1]
    own, other = own_ref[...], other_ref[...]
    out_ref[:, :half] = jnp.where(core == 0, own, other)
    out_ref[:, half:] = jnp.where(core == 0, other, own)


def blank_kernel(_, out_ref):
    out_ref[...] = jnp.zeros_like(out_ref)


def first_join_kernel(own_ref, other_ref, _, out_ref, packed_ref):
    join_kernel(own_ref, other_ref, out_ref)
    width = out_ref.shape[0]
    for i in range(C // LANES):
        packed_ref[i * width : (i + 1) * width] = out_ref[:, i * LANES : (i + 1) * LANES]


def unpack_kernel(*refs):
    out_ref = refs[-1]
    width = refs[0].shape[0] * LANES // C
    for at, ref in enumerate(refs[:-1]):
        for i in range(C // LANES):
            out_ref[at * width : (at + 1) * width, i * LANES : (i + 1) * LANES] = ref[i * width : (i + 1) * width]


def gather_tokens(own, packed):
    frames, rows = lax.axis_size("frames"), lax.axis_size("rows")
    if frames == 4 and rows == 2:
        far = [swap(packed, lambda f, r, c, d=d: (f ^ d, r ^ c, c)) for d in (3, 2, 1)]
        (rest,) = call(unpack_kernel, far, [((3 * own.shape[0], C), BF16)], flops=REST)
        return [own, swap_bit(own, "rows", 1)], [rest]
    parts = [own]
    for axis, count in (("frames", frames), ("rows", rows)):
        assert count & (count - 1) == 0
        bit = 1
        while bit < count:
            held = parts[0]
            if len(parts) > 1:
                shape = (2 * held.shape[0], C)
                (held,) = call(stack_kernel, parts, [(shape, BF16)], flops=JOIN)
            parts = [held, swap_bit(held, axis, bit)]
            bit *= 2
    return parts, []


def halves(core, half):
    own = pl.multiple_of(core * half, 16)
    return pl.ds(own, half), pl.ds(pl.multiple_of(half - own, 16), half)


def beside(refs, w_ref, channels, frames):
    frame = lax.axis_index("frames")
    terms = None
    for parity, ref in enumerate(refs):
        after = lax.rem(frame, 2) == parity
        there = jnp.where(after, frame < frames - 1, frame > 0)
        near = ref[...]
        near = jnp.where(there, near, jnp.zeros_like(near))
        term = jnp.dot(near, w_ref[jnp.where(after, 2, 0), channels], preferred_element_type=F32)
        terms = term if terms is None else terms + term
    return terms


def middle_kernel(own_ref, other_ref, w_ref, acc_ref, full):
    join_kernel(own_ref, other_ref, full)
    whole = full[...]
    acc_ref[...] = whole.astype(F32) + jnp.dot(whole, w_ref[1], preferred_element_type=F32)


def weights_kernel(wq_ref, wk_ref, wv_ref, wo_ref, held_ref, out_ref):
    core = lax.axis_index("heads")
    half = wo_ref.shape[0]
    for i, ref in enumerate((wq_ref, wk_ref, wv_ref)):
        held_ref[i * half : (i + 1) * half] = ref[...]
    for which in range(2):

        @pl.when(core == which)
        def _(keep=slice(which * half, (which + 1) * half), send=slice((1 - which) * half, (2 - which) * half)):
            out_ref[...] = wo_ref[:, keep]
            held_ref[3 * half :, :half] = wo_ref[: half // 2, send]
            held_ref[3 * half :, half:] = wo_ref[half // 2 :, send]


def first_kernel(frames, acc_ref, even_ref, odd_ref, w_ref, sum_ref):
    own = halves(lax.axis_index("heads"), even_ref.shape[1])[0]
    sum_ref[...] = acc_ref[...] + beside((even_ref, odd_ref), w_ref, own, frames)


def query_kernel(frames, acc_ref, even_ref, odd_ref, w_ref, held_ref, met_ref, gain_ref, temporal_ref, query_ref):
    core = lax.axis_index("heads")
    half = held_ref.shape[1] // 2
    other = halves(core, half)[1]
    temporal = (acc_ref[...] + beside((even_ref, odd_ref), w_ref, other, frames)).astype(BF16)
    temporal_ref[...] = jnp.where(core == 0, temporal[:, :half], temporal[:, half:])
    feats = temporal.astype(F32)
    centre = jnp.mean(feats, axis=-1, keepdims=True)
    centred = feats - centre
    spread = jnp.mean(centred * centred, axis=-1, keepdims=True)
    normed = (centred * lax.rsqrt(spread + EPS) * gain_ref[...]).astype(BF16)
    scale = (C // HEADS) ** -0.5
    query_ref[:half] = (nt_dot(held_ref[:half], normed) * scale).astype(BF16)
    query_ref[half:] = (nt_dot(met_ref[:half], normed) * scale).astype(BF16)


def attend_kernel(parts, *refs):
    blocks, refs = refs[:parts], refs[parts:]
    query_ref, temporal_ref, held_ref, met_ref, wo_ref, out_ref, tokens, keys, values, attended, out_weights = refs
    half = held_ref.shape[1] // 2
    size = C // HEADS
    at = 0
    for ref in blocks:
        tokens[at : at + ref.shape[0]] = ref[...]
        at += ref.shape[0]
    toks = tokens[...]
    wk, wv = (
        jnp.concatenate([ref[i * half : (i + 1) * half] for ref in (held_ref, met_ref)], axis=0) for i in (1, 2)
    )
    values[...] = nt_dot(wv, toks).astype(BF16)
    found = nt_dot(toks, wk).astype(BF16)
    for head in range(HEADS):
        keys[head, :, :size] = found[:, head * size : (head + 1) * size]
    probs = []
    for head in range(HEADS):
        rows = slice(head * size, (head + 1) * size)
        scores = jnp.dot(keys[head, :, :size], query_ref[rows], preferred_element_type=F32)
        expo = jnp.exp(scores - jnp.max(scores, axis=0, keepdims=True))
        probs.append((expo.astype(BF16), 1.0 / jnp.sum(expo, axis=0, keepdims=True)))
    for head in range(HEADS):
        rows = slice(head * size, (head + 1) * size)
        prob, inverse = probs[head]
        mixed = jnp.dot(values[rows], prob, preferred_element_type=F32)
        attended[rows] = (mixed * inverse).astype(BF16)
    out_weights[:half] = wo_ref[...]
    out_weights[half : half + half // 2] = met_ref[3 * half :, :half]
    out_weights[half + half // 2 :] = met_ref[3 * half :, half:]
    mixed = tn_dot(attended[...], out_weights[...])
    out_ref[...] = (temporal_ref[...].astype(F32) + mixed).astype(BF16)


def body(clip_latent, norm_gain, w_time, w_query, w_key, w_value, w_out, reference_tokens):
    frames_here, rows_here, cols_here, half = clip_latent.shape
    assert frames_here == 1 and lax.axis_size("heads") == 2
    places = rows_here * cols_here
    width = reference_tokens.shape[0]
    clip = clip_latent.reshape(places, half)
    frames = lax.axis_size("frames")
    frames = lax.axis_size("frames")
    clip_other, toks_other = sibling(clip), sibling(reference_tokens)
    clip_other, toks_other = lax.optimization_barrier((clip_other, toks_other))
    even, odd = swap_frames(clip, 0), swap_frames(clip, 1)
    even_other, odd_other = sibling(even), sibling(odd)
    (blank,) = call(blank_kernel, (toks_other,), [((8, 128), F32)], flops=AHEAD)
    own, packed = call(
        first_join_kernel,
        (reference_tokens, toks_other, blank),
        [((width, C), BF16), ((width * C // LANES, LANES), BF16)],
        flops=JOIN,
    )
    toks, rest = gather_tokens(own, packed)
    (acc,) = call(
        middle_kernel,
        (clip, clip_other, w_time),
        [((places, C), F32)],
        [pltpu.VMEM((places, C), BF16)],
        flops=MIDDLE,
    )
    *wide, _ = lax.optimization_barrier((w_query.T, w_key.T, w_value.T, w_out, acc))
    held, wo = call(weights_kernel, wide, [((7 * half // 2, C), BF16), ((half, half), BF16)], flops=WEIGHTS)
    met = sibling(held)
    (acc,) = call(
        functools.partial(first_kernel, frames), (acc, even, odd, w_time), [((places, C), F32)], flops=FIRST
    )
    temporal, query = call(
        functools.partial(query_kernel, frames),
        (acc, even_other, odd_other, w_time, held, met, norm_gain),
        [((places, half), BF16), ((C, places), BF16)],
        flops=QUERY,
    )
    for part in rest:
        toks += [part, sibling(part)]
    count = width * frames * lax.axis_size("rows")
    (out,) = call(
        functools.partial(attend_kernel, len(toks)),
        (*toks, query, temporal, held, met, wo),
        [((places, half), BF16)],
        [
            pltpu.VMEM((count, C), BF16),
            pltpu.VMEM((HEADS, count, 128), BF16),
            pltpu.VMEM((C, count), BF16),
            pltpu.VMEM((C, places), BF16),
            pltpu.VMEM((C, half), BF16),
        ],
        flops=ATTEND,
    )
    return out.reshape(clip_latent.shape)


def solution(mesh):
    return jax.shard_map(
        body,
        mesh=mesh,
        in_specs=(
            P(("groups", "frames"), "rows", None, "heads"),
            P(),
            P(),
            P(None, "heads"),
            P(None, "heads"),
            P(None, "heads"),
            P("heads", None),
            P(("groups", "frames", "rows"), "heads"),
        ),
        out_specs=P(("groups", "frames"), "rows", None, "heads"),
        check_vma=False,
    )
```
